32 devices in a mesh: tok: 8 (over z, x), head: 4 (over y, core).
Axes of the slice: x: 2, y: 2, z: 4, core: 2. Of those that a mesh axis runs over, the one named last changes fastest.
Arguments:
- tokens: bfloat16 [4096, 1664], P(('tok', 'head')), may hold values from -75 to 75
- attn_gain: float32 [1664], replicated, may hold values from 0.1 to 1.9
- qkv_weight: bfloat16 [3, 1664, 1664], P(None, 'head'), may hold values from -5 to 5
- out_weight: bfloat16 [1664, 1664], P('head'), may hold values from -0.4375 to 0.4375
- merge_gain: float32 [1664], replicated, may hold values from 0.1 to 1.9
- merge_weight: bfloat16 [6656, 4096], P('head', 'tok'), may hold values from -0.078125 to 0.078125
- grid_sizes: int32 [2, 16], P(None, 'tok'), may hold values from 2 to 16, as said below
- segment_ids: int32 [4096], P('tok'), may hold values from 0 to 15, as said below
- patch_pos: int32 [2, 4096], P(None, 'tok'), may hold values from 0 to 15, as said below
- live_mask: int32 [4096], P('tok'), may hold values from 0 to 1, as said below
- owners: int32 [1024, 1], P(('tok', 'head')), may hold values from 0 to 7; in each aligned block of 32 rows (0 to 31, 32 to 63, ...) at most 8 rows name the same one
Outputs:
- delivered: bfloat16 [2048, 4096], P(('tok', 'head'))
The draws below stay inside these ranges and needn't reach their ends.
Inputs may be any that keep to these rules, and one draw needn't show every extreme that they name: `grid_sizes`: both sides of every image are even, and some image is 16 by 16. `segment_ids`: never fall along the tokens. The aligned block b of 512 tokens holds images b * 2 to (b + 1) * 2 - 1 packed in order from the block's start, image s taking grid_sizes[0, s] * grid_sizes[1, s] tokens; the block's remaining tokens carry the number of its last image. `patch_pos`: an image's tokens come in 2x2 windows, windows in row-major order, each window as (2 * r, 2 * c), (2 * r, 2 * c + 1), (2 * r + 1, 2 * c), (2 * r + 1, 2 * c + 1); padding tokens sit at (0, 0). `live_mask`: 1 exactly on the tokens that belong to an image. `owners`: in each aligned block of 32 rows (the merged rows of one device) no owner is named more than 8 times.
All inputs are finite; a program needn't handle non-finite values.
Results may differ from the reference program's by a relative error of at most 0.024.
Values may be sent and summed in bfloat16 or wider, within the bound.
A program may use at most 64 MiB of HBM per device.

```python
import math
import jax
import jax.numpy as jnp
import numpy as np
from jax import lax

D = 1664
HEADS = 16
HD = 104
OUT = 4096
SIDE = 16
GROUP = 512
TOKENS = 4096
IMG_GRP = 2
MDEV = 32
MERGED = 1024
CAP = 8
SLOTS = 64
N_TOK = 8
N_HEAD = 4


def packing(key):
    base_key = jax.random.fold_in(key, 31)
    half_side = SIDE // 2
    half_low = max(1, 3 * SIDE // 8)
    heights = 2 * jax.random.randint(jax.random.fold_in(base_key, 1), (N_TOK, IMG_GRP), half_low, half_side + 1, dtype=jnp.int32)
    widths = 2 * jax.random.randint(jax.random.fold_in(base_key, 2), (N_TOK, IMG_GRP), half_low, half_side + 1, dtype=jnp.int32)
    heights = heights.at[0, 0].set(SIDE)
    widths = widths.at[0, 0].set(SIDE)
    image_area = heights * widths
    starts = jnp.cumsum(image_area, axis=1, dtype=jnp.int32) - image_area
    totals = jnp.sum(image_area, axis=1, dtype=jnp.int32)
    places = jnp.arange(GROUP, dtype=jnp.int32)
    started = (starts[:, None, :] <= places[None, :, None]).astype(jnp.int32)
    image_slot = jnp.sum(started, axis=2, dtype=jnp.int32) - 1
    slot_hot = (image_slot[:, :, None] == jnp.arange(IMG_GRP, dtype=jnp.int32)[None, None, :]).astype(jnp.int32)
    own_start = jnp.sum(slot_hot * starts[:, None, :], axis=2, dtype=jnp.int32)
    own_width = jnp.sum(slot_hot * widths[:, None, :], axis=2, dtype=jnp.int32)
    live_flag = (places[None, :] < totals[:, None]).astype(jnp.int32)
    offset = places[None, :] - own_start
    window = offset // 4
    within = offset % 4
    window_cols = own_width // 2
    row_pos = (2 * (window // window_cols) + within // 2) * live_flag
    col_pos = (2 * (window % window_cols) + within % 2) * live_flag
    segments = jnp.arange(N_TOK, dtype=jnp.int32)[:, None] * IMG_GRP + image_slot
    grid_table = jnp.stack([heights.reshape(-1), widths.reshape(-1)])
    positions = jnp.stack([row_pos.reshape(-1), col_pos.reshape(-1)])
    return (grid_table, segments.reshape(-1), positions, live_flag.reshape(-1))


def draw_grid_sizes(key, part):
    return packing(key)[0]


def draw_segment_ids(key, part):
    return packing(key)[1]


def draw_patch_pos(key, part):
    return packing(key)[2]


def draw_live_mask(key, part):
    return packing(key)[3]


def draw_tokens(key, part):
    key_noise, key_rows, key_cols = jax.random.split(key, 3)
    row_scale = jnp.exp(jax.random.uniform(key_rows, (TOKENS, 1), jnp.float32, math.log(0.5), math.log(5.0)))
    feature_ramp = 1.0 + 2.0 * jnp.arange(D, dtype=jnp.float32) / (D - 1)
    col_scale = jnp.exp(jax.random.uniform(key_cols, (1, D), jnp.float32, math.log(0.4), math.log(1.2))) * feature_ramp[None, :]
    base_noise = jnp.clip(jax.random.normal(key_noise, (TOKENS, D), jnp.float32), -4.0, 4.0)
    return (base_noise * row_scale * col_scale).astype(jnp.bfloat16)


def draw_qkv_weight(key, part):
    key_main = jax.random.fold_in(key, 0)
    weights = jnp.clip(jax.random.normal(key_main, (3, D, D), jnp.float32), -6.0, 6.0) / math.sqrt(D)
    return weights.astype(jnp.bfloat16)


def shard_levels(key, dims, shards, smallest, high):
    loudness, own = 1.0, jax.random.fold_in(key, 6)
    for position, shards_of in shards:
        steps = jnp.exp(jax.random.uniform(jax.random.fold_in(own, position), (shards_of,), jnp.float32, smallest / len(shards), high / len(shards)))
        loudness = loudness * jnp.repeat(steps, dims[position] // shards_of).reshape([-1 if axis == position else 1 for axis in range(len(dims))])
    return loudness


def routed_block(own_key, own, number, rows, amount, top, limit, slope):
    order = jax.random.permutation(own_key, amount)
    crowded, usual = load_shares(amount, rows * top, limit, slope, True), load_shares(amount, rows * top, limit, slope, False)
    places = jnp.arange(amount)

    def named(sizes, rotation):
        used = int((sizes > 0).sum())
        fixed = max(1, used // 4)
        moved = fixed + (places - fixed + rotation * (used - fixed)) % max(1, amount - fixed)
        return jnp.zeros((amount,), jnp.int32).at[order[jnp.where(places < fixed, places, moved)]].set(jnp.asarray(sizes, jnp.int32))

    sizes = jnp.where(number % 4 == 0, named(crowded, number // 4), named(usual, number - number // 4 - 1))
    mixed = jax.random.permutation(jax.random.fold_in(own, 3), amount)
    giver, receiver = mixed[0:amount // 2 * 2:2], mixed[1:amount // 2 * 2:2]
    room = jnp.minimum(sizes[giver] - 1, limit - sizes[receiver]) // 2
    room = jnp.where((giver == order[0]) | (receiver == order[0]) | (sizes[receiver] == 0), 0, jnp.maximum(room, 0))
    moved = jax.random.randint(jax.random.fold_in(own, 4), (amount // 2,), 0, 1 << 20) % (room + 1)
    sizes = sizes.at[giver].add(-moved).at[receiver].add(moved)
    labels = jnp.searchsorted(jnp.cumsum(sizes), jnp.arange(rows * top), side="right").astype(jnp.int32)
    grid = labels.reshape(top, rows).T
    grid = grid[jax.random.permutation(jax.random.fold_in(own, 1), rows)]
    rotation = jax.random.randint(jax.random.fold_in(own, 2), (rows, 1), 0, top)
    return jnp.take_along_axis(grid, (jnp.arange(top)[None, :] + rotation) % top, axis=1)


def load_shares(amount, total, most, slope, full):
    loads = [(1 << 20) // math.isqrt(grade ** slope) + 1 for grade in range(1, amount + 1)]
    largest = most if full else min(most, max(-(-total // amount), total * loads[0] // sum(loads)))
    least = 1 if total - largest >= amount - 1 else 0
    counts, rest = [largest] + [least] * (amount - 1), total - largest - least * (amount - 1)
    while rest > 0:
        movable = [i for i in range(1, amount) if counts[i] < largest] or [i for i in range(1, amount) if counts[i] < most]
        whole, remaining = sum([loads[i] for i in movable]), rest
        for i in movable:
            addition = min(most - counts[i], max(1, remaining * loads[i] // whole), rest)
            counts[i] = counts[i] + addition
            rest = rest - addition
    return np.array(counts)


def scatter_about(own_key, extent, width, limit, cuts=(), kind=jnp.bfloat16):
    result = width * jax.random.normal(own_key, extent, jnp.float32)
    if cuts:
        result = result * shard_levels(own_key, extent, cuts, -0.22, 0.18)
    return jnp.clip(result, -limit, limit).astype(kind)


def setup_inputs(seed: int = 0) -> dict:
    streams_of = jax.random.split(jax.random.key(seed), 12)
    tokens = draw_tokens(jax.random.fold_in(streams_of[11], 71), 0)
    attn_gain = jnp.clip(1.0 + 0.18 * jax.random.normal(streams_of[1], (D,), jnp.float32), 0.1, 1.9)
    qkv_weight = draw_qkv_weight(jax.random.fold_in(streams_of[11], 71), 0)
    out_weight = scatter_about(streams_of[3], (D, D), (2 * HD) ** -0.5, 0.4375, ((0, 4),))
    merge_gain = jnp.clip(1.0 + 0.18 * jax.random.normal(streams_of[4], (D,), jnp.float32), 0.1, 1.9)
    merge_weight = scatter_about(streams_of[5], (4 * D, OUT), (4 * D) ** -0.5, 0.078125, ((0, 4), (1, 8)))
    grid_sizes = draw_grid_sizes(jax.random.fold_in(streams_of[11], 71), 0)
    segment_ids = draw_segment_ids(jax.random.fold_in(streams_of[11], 71), 0)
    patch_pos = draw_patch_pos(jax.random.fold_in(streams_of[11], 71), 0)
    live_mask = draw_live_mask(jax.random.fold_in(streams_of[11], 71), 0)
    owners_keys = jax.random.split(jax.random.fold_in(streams_of[10], 1), MERGED // MDEV)
    owners_turns = jax.random.permutation(jax.random.fold_in(streams_of[10], 3), MERGED // MDEV)
    owners = jax.vmap(lambda own, number: routed_block(jax.random.fold_in(streams_of[10], 2), own, number, MDEV, N_TOK, 1, CAP, 2))(owners_keys, owners_turns).reshape((MERGED, 1))
    return dict(tokens=tokens, attn_gain=attn_gain, qkv_weight=qkv_weight, out_weight=out_weight, merge_gain=merge_gain, merge_weight=merge_weight, grid_sizes=grid_sizes, segment_ids=segment_ids, patch_pos=patch_pos, live_mask=live_mask, owners=owners)


EPSILON = 1e-06
NEGATIVE = -1e+30

def layer_norm(values, gain_vec):
    average = lax.optimization_barrier(jnp.mean(values, axis=-1, keepdims=True))
    centred = values - average
    variance = lax.optimization_barrier(jnp.mean(centred * centred, axis=-1, keepdims=True))
    return centred * lax.rsqrt(variance + EPSILON) * gain_vec

def rotate(vectors, row_coord, col_coord):
    quarter = vectors.shape[-1] // 4
    frequency = 10000.0 ** (-jnp.arange(quarter, dtype=jnp.float32) / quarter)
    pieces = []
    for which_axis, coordinate in ((0, row_coord), (1, col_coord)):
        leading = vectors[..., 2 * which_axis * quarter:(2 * which_axis + 1) * quarter]
        trailing = vectors[..., (2 * which_axis + 1) * quarter:(2 * which_axis + 2) * quarter]
        angles = coordinate[:, None, None] * frequency
        cosine = jnp.cos(angles)
        sine_val = jnp.sin(angles)
        pieces.append(leading * cosine - trailing * sine_val)
        pieces.append(leading * sine_val + trailing * cosine)
    return jnp.concatenate(pieces, axis=-1)

def attend(queries, key_rows, value_rows, segments, live_flag):
    positions = jnp.arange(segments.shape[0], dtype=jnp.int32)
    allowed = (segments[:, None] == segments[None, :]) & ((live_flag[None, :] == 1) | (positions[:, None] == positions[None, :]))

    def one_head(head_data):
        query_head, key_head, value_head = head_data
        scores = jnp.dot(query_head, key_head.T, preferred_element_type=jnp.float32)
        masked = jnp.where(allowed, scores, NEGATIVE)
        row_top = lax.optimization_barrier(jnp.max(masked, axis=1, keepdims=True))
        exponent = jnp.where(allowed, jnp.exp(masked - row_top), 0.0)
        denominator = lax.optimization_barrier(jnp.sum(exponent, axis=1, keepdims=True))
        numerator = jnp.dot(exponent.astype(jnp.bfloat16), value_head, preferred_element_type=jnp.float32)
        return (numerator / denominator).astype(jnp.bfloat16)
    stacked = (jnp.swapaxes(queries, 0, 1), jnp.swapaxes(key_rows, 0, 1), jnp.swapaxes(value_rows, 0, 1))
    return jnp.swapaxes(lax.map(one_head, stacked), 0, 1)

def reference(tokens, attn_gain, qkv_weight, out_weight, merge_gain, merge_weight, grid_sizes, segment_ids, patch_pos, live_mask, owners):
    picked = grid_sizes[:, segment_ids].astype(jnp.float32)
    coords = patch_pos.astype(jnp.float32) * SIDE / picked
    head_width = HEADS // N_HEAD * HD
    stacked_weight = qkv_weight.reshape(3 * D, D)

    def one_group(group_data):
        group_tokens, group_coords, group_segments, group_live = group_data
        normed = layer_norm(group_tokens.astype(jnp.float32), attn_gain).astype(jnp.bfloat16)
        projected_rows = lax.dot_general(normed, stacked_weight, (((1,), (1,)), ((), ())), preferred_element_type=jnp.float32).reshape(GROUP, 3, HEADS, HD)
        queries = (rotate(projected_rows[:, 0], group_coords[0], group_coords[1]) * HD ** (-0.5)).astype(jnp.bfloat16)
        key_rows = rotate(projected_rows[:, 1], group_coords[0], group_coords[1]).astype(jnp.bfloat16)
        value_rows = projected_rows[:, 2].astype(jnp.bfloat16)
        heads_out = attend(queries, key_rows, value_rows, group_segments, group_live).reshape(GROUP, D)
        attn_out = jnp.zeros((GROUP, D), jnp.float32)
        for member in range(N_HEAD):
            columns = heads_out[:, member * head_width:(member + 1) * head_width]
            head_term = jnp.dot(columns, out_weight[member * head_width:(member + 1) * head_width], preferred_element_type=jnp.float32)
            attn_out = attn_out + lax.optimization_barrier(head_term.astype(jnp.bfloat16)).astype(jnp.float32)
        stream = (group_tokens.astype(jnp.float32) + attn_out).reshape(GROUP // 4, 4, D)
        average = lax.optimization_barrier(jnp.mean(stream, axis=2, keepdims=True))
        variance = lax.optimization_barrier(jnp.mean(stream * stream, axis=2, keepdims=True)) - average * average
        normal_rows = (stream - average) * lax.rsqrt(variance + EPSILON) * merge_gain
        return normal_rows.astype(jnp.bfloat16).reshape(GROUP // 4, 4 * D)
    group_inputs = (tokens.reshape(N_TOK, GROUP, D), jnp.transpose(coords.reshape(2, N_TOK, GROUP), (1, 0, 2)), segment_ids.reshape(N_TOK, GROUP), live_mask.reshape(N_TOK, GROUP))
    merged = lax.map(one_group, group_inputs).reshape(MERGED, 4 * D)
    slice_width = 4 * D // N_HEAD
    summed = jnp.zeros((MERGED, OUT), jnp.float32)
    for member in range(N_HEAD):
        head_term = jnp.dot(merged[:, member * slice_width:(member + 1) * slice_width], merge_weight[member * slice_width:(member + 1) * slice_width], preferred_element_type=jnp.float32)
        summed = summed + lax.optimization_barrier(head_term.astype(jnp.bfloat16)).astype(jnp.float32)
    projected = summed.astype(jnp.bfloat16)
    block_rows = projected.reshape(N_TOK, N_HEAD, MDEV, OUT).astype(jnp.float32)
    owner_block = owners[:, 0].reshape(N_TOK, N_HEAD, MDEV)
    owner_hot = (owner_block[..., None] == jnp.arange(N_TOK, dtype=jnp.int32)).astype(jnp.int32)
    earlier = jnp.cumsum(owner_hot, axis=2, dtype=jnp.int32) - owner_hot
    slot_index = lax.optimization_barrier(jnp.sum(earlier * owner_hot, axis=3, dtype=jnp.int32))
    slot_hot = (slot_index[..., None] == jnp.arange(CAP, dtype=jnp.int32)).astype(jnp.float32)
    select = owner_hot.astype(jnp.float32)[..., None] * slot_hot[:, :, :, None, :]
    delivered = jnp.einsum('thmoc,thmf->ohtcf', select, block_rows, precision=lax.Precision.HIGHEST)
    return delivered.reshape(N_TOK * N_HEAD * SLOTS, OUT).astype(jnp.bfloat16)
```

```python
import jax
import jax.numpy as jnp
from jax import lax
from jax.experimental import pallas as pl
from jax.experimental.pallas import tpu as pltpu
from jax.sharding import PartitionSpec as P

D = 1664
HD = 104
SIDE = 16


EPSILON = 1e-06
NEGATIVE = -1e30


def layer_norm(values, gain_vec):
    average = jnp.mean(values, axis=-1, keepdims=True)
    centred = values - average
    variance = jnp.mean(centred * centred, axis=-1, keepdims=True)
    return centred * lax.rsqrt(variance + EPSILON) * gain_vec


def rotate(vectors, row_coord, col_coord):
    quarter = vectors.shape[-1] // 4
    frequency = 10000.0 ** (-jnp.arange(quarter, dtype=jnp.float32) / quarter)
    pieces = []
    for which_axis, coordinate in ((0, row_coord), (1, col_coord)):
        leading = vectors[..., 2 * which_axis * quarter : (2 * which_axis + 1) * quarter]
        trailing = vectors[..., (2 * which_axis + 1) * quarter : (2 * which_axis + 2) * quarter]
        angles = coordinate[:, None, None] * frequency
        cosine = jnp.cos(angles)
        sine_val = jnp.sin(angles)
        pieces.append(leading * cosine - trailing * sine_val)
        pieces.append(leading * sine_val + trailing * cosine)
    return jnp.concatenate(pieces, axis=-1)


def earlier_rows(owner_col):
    places = jnp.arange(owner_col.shape[0], dtype=jnp.int32)
    same = (owner_col[:, None] == owner_col[None, :]) & (places[None, :] < places[:, None])
    return jnp.sum(same.astype(jnp.int32), axis=1, dtype=jnp.int32)


def body(
    tokens,
    attn_gain,
    qkv_weight,
    out_weight,
    merge_gain,
    merge_weight,
    grid_sizes,
    segment_ids,
    patch_pos,
    live_mask,
    owners,
):
    group_len = segment_ids.shape[0]
    local_rows = tokens.shape[0]
    head_width = qkv_weight.shape[1]
    heads_here = head_width // HD
    tok_count = lax.axis_size("tok")
    image_count = grid_sizes.shape[1]
    local_image = segment_ids - lax.axis_index("tok") * image_count
    image_match = local_image[:, None] == jnp.arange(image_count, dtype=jnp.int32)[None, :]
    grid_float = grid_sizes.astype(jnp.float32)
    row_size = jnp.sum(jnp.where(image_match, grid_float[0][None, :], 0.0), axis=1)
    col_size = jnp.sum(jnp.where(image_match, grid_float[1][None, :], 0.0), axis=1)
    row_coord = patch_pos[0].astype(jnp.float32) * SIDE / row_size
    col_coord = patch_pos[1].astype(jnp.float32) * SIDE / col_size
    stacked_weight = qkv_weight.reshape(3 * head_width, D)
    normed = layer_norm(tokens.astype(jnp.float32), attn_gain).astype(jnp.bfloat16)
    projected_rows = lax.dot_general(
        lax.all_gather(normed, "head", axis=0, tiled=True),
        stacked_weight,
        (((1,), (1,)), ((), ())),
        preferred_element_type=jnp.float32,
    )
    projected_rows = projected_rows.reshape(group_len, 3, heads_here, HD)
    query_all = (rotate(projected_rows[:, 0], row_coord, col_coord) * HD ** (-0.5)).astype(
        jnp.bfloat16
    )
    key_all = rotate(projected_rows[:, 1], row_coord, col_coord).astype(jnp.bfloat16)
    value_all = projected_rows[:, 2].astype(jnp.bfloat16)
    block_len = min(512, group_len)
    block_count = group_len // block_len
    key_live = live_mask == 1

    def allowed_pairs(query_start, span):
        query_seg = lax.dynamic_slice_in_dim(segment_ids, query_start, block_len)
        query_place = query_start + jnp.arange(block_len, dtype=jnp.int32)
        key_place = jnp.arange(span, dtype=jnp.int32)
        same_image = query_seg[:, None] == segment_ids[None, :]
        return same_image & (key_live[None, :] | (query_place[:, None] == key_place[None, :]))

    def query_block(query_start):
        queries = lax.dynamic_slice_in_dim(query_all, query_start, block_len, 0)
        allowed = allowed_pairs(query_start, group_len)
        scores = jnp.einsum("qhd,khd->hqk", queries, key_all, preferred_element_type=jnp.float32)
        masked = jnp.where(allowed[None], scores, NEGATIVE)
        row_top = jnp.max(masked, axis=2, keepdims=True)
        exponent = jnp.where(allowed[None], jnp.exp(masked - row_top), 0.0)
        denominator = jnp.sum(exponent, axis=2)
        numerator = jnp.einsum(
            "hqk,khd->qhd",
            exponent.astype(jnp.bfloat16),
            value_all,
            preferred_element_type=jnp.float32,
        )
        return (numerator / denominator.T[:, :, None]).astype(jnp.bfloat16)

    block_starts = jnp.arange(block_count, dtype=jnp.int32) * block_len
    heads_out = lax.map(query_block, block_starts).reshape(group_len, head_width)
    attn_rows = lax.psum_scatter(
        jnp.dot(heads_out, out_weight, preferred_element_type=jnp.float32).astype(jnp.bfloat16),
        "head",
        scatter_dimension=0,
        tiled=True,
    ).astype(jnp.float32)
    stream = (tokens.astype(jnp.float32) + attn_rows).reshape(local_rows // 4, 4, D)
    average = jnp.sum(stream, axis=2, keepdims=True) / D
    variance = jnp.sum(stream * stream, axis=2, keepdims=True) / D - average * average
    window_rows = ((stream - average) * lax.rsqrt(variance + EPSILON) * merge_gain).astype(
        jnp.bfloat16
    )
    merged_slice = lax.all_to_all(
        window_rows.reshape(local_rows // 4, 4 * D), "head", split_axis=1, concat_axis=0, tiled=True
    )
    merged_count = local_rows // 4
    column_terms = jnp.dot(
        merged_slice,
        lax.all_gather(merge_weight, "tok", axis=1, tiled=True),
        preferred_element_type=jnp.float32,
    )
    projected = lax.psum_scatter(
        column_terms.astype(jnp.bfloat16), "head", scatter_dimension=0, tiled=True
    )
    slot_count = max(2, 2 * merged_count // tok_count)
    owner_col = owners[:, 0]
    slot_index = earlier_rows(owner_col)
    target = owner_col * slot_count + slot_index
    select = (
        jnp.arange(tok_count * slot_count, dtype=jnp.int32)[:, None] == target[None, :]
    ).astype(jnp.bfloat16)
    send_rows = jnp.dot(select, projected, preferred_element_type=jnp.float32).astype(jnp.bfloat16)
    send_rows = send_rows.reshape(tok_count, slot_count, -1)
    received = lax.all_to_all(send_rows, "tok", split_axis=0, concat_axis=0, tiled=True)
    return received.reshape(tok_count * slot_count, -1)


VMEM_SPEC = pl.BlockSpec(memory_space=pltpu.VMEM)
MESH = pl.DeviceIdType.MESH
VMEM_LIMIT = 48 * 1024 * 1024


def remote(source, target, send, arrive, tok, head):
    return pltpu.make_async_remote_copy(
        src_ref=source,
        dst_ref=target,
        send_sem=send,
        recv_sem=arrive,
        device_id=(tok, head),
        device_id_type=MESH,
    )


def greet(devices):
    barrier = pltpu.get_barrier_semaphore()
    for device in devices:
        pl.semaphore_signal(barrier, inc=1, device_id=device, device_id_type=MESH)
    pl.semaphore_wait(barrier, len(devices))


def head_partners():
    tok, head = lax.axis_index("tok"), lax.axis_index("head")
    sibling = head + 1 - 2 * (head % 2)
    across = (head + 2) % 4
    return tok, head, sibling, across


def gather_kernel(
    tokens_ref, gain_ref, normed_ref, residual_ref, raw, own_sems, across_sems, relay_sems
):
    tok, head, sibling, across = head_partners()
    diagonal = (sibling + 2) % 4
    parts = tokens_ref.shape[0]
    greet([(tok, sibling), (tok, across)])

    def to_across(r):
        return remote(
            tokens_ref.at[r], raw.at[1, r], across_sems.at[0, r], across_sems.at[1, r], tok, across
        )

    def to_sibling(r):
        return remote(
            tokens_ref.at[r], raw.at[0, r], own_sems.at[0, r], own_sems.at[1, r], tok, sibling
        )

    def relay(r):
        return remote(
            raw.at[1, r], raw.at[2, r], relay_sems.at[0, r], relay_sems.at[1, r], tok, sibling
        )

    def settle(rows, r, source):
        values = rows.astype(jnp.float32)
        average = jnp.mean(values, axis=-1, keepdims=True)
        centred = values - average
        variance = jnp.mean(centred * centred, axis=-1, keepdims=True)
        normal = centred * lax.rsqrt(variance + EPSILON) * gain_ref[...]
        normed_ref[r, source] = normal.astype(jnp.bfloat16)

    for r in range(parts):
        to_across(r).start()
    for r in range(parts):
        to_sibling(r).start()

    @pl.loop(0, parts)
    def _(r):
        settle(tokens_ref[r], r, head)

    @pl.loop(0, parts)
    def _(r):
        to_sibling(r).wait_recv()
        settle(raw[0, r], r, sibling)

    @pl.loop(0, parts)
    def _(r):
        to_across(r).wait_recv()
        relay(r).start()
        settle(raw[1, r], r, across)

    @pl.loop(0, parts)
    def _(r):
        relay(r).wait_recv()
        settle(raw[2, r], r, diagonal)

    residual_ref[head] = tokens_ref[head]
    residual_ref[sibling] = raw[0, head]
    residual_ref[across] = raw[1, head]
    residual_ref[diagonal] = raw[2, head]

    @pl.loop(0, parts)
    def _(r):
        to_across(r).wait_send()
        to_sibling(r).wait_send()
        relay(r).wait_send()


def merge_kernel(
    part_ref, residual_ref, gain_ref, weight_ref, other_ref, target_ref, out_ref,
    near_sum, sent_sum, far_sum, rows, terms, near_term, sent_term, far_term, places, messages,
    sum_near_sems, sum_far_sems, row_x_sems, row_z_sems, row_relay_sems,
    term_near_sems, term_far_sems, place_sems, out_sems, local_sems,
):
    tok, head, sibling, across = head_partners()
    diagonal = (sibling + 2) % 4
    toks = lax.axis_size("tok")
    p, q, x = tok // 4, (tok // 2) % 2, tok % 2
    beside = tok + 1 - 2 * x
    over = (tok + 4) % 8
    corner = (beside + 4) % 8
    span = near_sum.shape[2]
    chunks = part_ref.shape[1]
    owned = near_term.shape[2]
    half = weight_ref.shape[1]
    greet(
        [((tok + step) % toks, head) for step in range(1, toks)] + [(tok, sibling), (tok, across)]
    )

    def near_copy(c, which):
        block = (diagonal, sibling)[which]
        return remote(
            part_ref.at[block, c], near_sum.at[which, c],
            sum_near_sems.at[0, which, c], sum_near_sems.at[1, which, c], tok, sibling,
        )

    def far_copy(c):
        return remote(
            sent_sum.at[c], far_sum.at[c], sum_far_sems.at[0, c], sum_far_sems.at[1, c], tok, across
        )

    for c in range(chunks):
        near_copy(c, 0).start()
    for c in range(chunks):
        near_copy(c, 1).start()
    place_copies = [
        remote(
            target_ref, places.at[k], place_sems.at[0, k], place_sems.at[1, k], device, head
        )
        for k, device in enumerate((beside, over, corner))
    ]
    for copy in place_copies:
        copy.start()

    @pl.loop(0, chunks)
    def _(c):
        near_copy(c, 0).wait_recv()
        total = part_ref[across, c].astype(jnp.float32) + near_sum[0, c].astype(jnp.float32)
        sent_sum[c] = total.astype(jnp.bfloat16)
        far_copy(c).start()

    def row_x(c):
        return remote(
            rows.at[0, c], rows.at[1, c], row_x_sems.at[0, c], row_x_sems.at[1, c], beside, head
        )

    def row_z(c):
        return remote(
            rows.at[0, c], rows.at[2, c], row_z_sems.at[0, c], row_z_sems.at[1, c], over, head
        )

    def row_relay(c):
        return remote(
            rows.at[2, c], rows.at[3, c],
            row_relay_sems.at[0, c], row_relay_sems.at[1, c], beside, head,
        )

    width = residual_ref.shape[-1]

    @pl.loop(0, chunks)
    def _(c):
        near_copy(c, 1).wait_recv()
        stream = residual_ref[c].astype(jnp.float32) + part_ref[head, c].astype(jnp.float32)
        stream = stream + near_sum[1, c].astype(jnp.float32)
        far_copy(c).wait_recv()
        stream = stream + far_sum[c].astype(jnp.float32)
        average = jnp.sum(stream, axis=-1, keepdims=True) / width
        variance = jnp.sum(stream * stream, axis=-1, keepdims=True) / width - average * average
        normal = (stream - average) * lax.rsqrt(variance + EPSILON) * gain_ref[...]
        rows[0, c] = normal.astype(jnp.bfloat16)
        row_z(c).start()
        row_x(c).start()

    own_columns = pl.ds(pl.multiple_of(q * half, half), half)
    other_columns = pl.ds(pl.multiple_of((1 - q) * half, half), half)

    def term_near(k, which):
        block = (diagonal, sibling)[which]
        return remote(
            terms.at[k, block], near_term.at[k, which],
            term_near_sems.at[0, k, which], term_near_sems.at[1, k, which], tok, sibling,
        )

    def term_far(k):
        return remote(
            sent_term.at[k], far_term.at[k], term_far_sems.at[0, k], term_far_sems.at[1, k],
            tok, across,
        )

    def project(k):
        block = rows[k].reshape(chunks * span, width)
        for weights, columns in ((weight_ref, own_columns), (other_ref, other_columns)):
            product = jnp.dot(block, weights[...], preferred_element_type=jnp.float32)
            product = product.astype(jnp.bfloat16).reshape(4, owned, half)
            terms[k, :, :, columns] = product
        term_near(k, 0).start()
        term_near(k, 1).start()

    def pass_on(k):
        term_near(k, 0).wait_recv()
        total = terms[k, across].astype(jnp.float32) + near_term[k, 0].astype(jnp.float32)
        sent_term[k] = total.astype(jnp.bfloat16)
        term_far(k).start()

    def projected(k):
        term_near(k, 1).wait_recv()
        total = terms[k, head].astype(jnp.float32) + near_term[k, 1].astype(jnp.float32)
        term_far(k).wait_recv()
        return (total + far_term[k].astype(jnp.float32)).astype(jnp.bfloat16)

    slots = messages.shape[2]

    def delivery(which, step):
        owner = (tok + step) % toks
        group = p if which == 0 else 1 - p
        return remote(
            messages.at[which, owner], out_ref.at[group, tok],
            out_sems.at[0, which, step], out_sems.at[1, which, step], owner, head,
        )

    def kept(which):
        group = p if which == 0 else 1 - p
        return pltpu.make_async_copy(
            messages.at[which, tok], out_ref.at[group, tok], local_sems.at[which]
        )

    def deliver(which):
        lines = lax.broadcasted_iota(jnp.int32, (toks * slots, owned), 0).astype(jnp.float32)
        sent = jnp.zeros((toks * slots, 2 * half), jnp.float32)
        for turn in range(2):
            k = 2 * which + turn
            aim = target_ref[0:1, 0:owned] if k == 0 else places[k - 1, 0:1, 0:owned]
            side = x if turn == 0 else 1 - x
            aim = aim + (side * (slots // 2)).astype(jnp.float32)
            chosen = jnp.where(lines == aim, 1.0, 0.0).astype(jnp.bfloat16)
            sent = sent + jnp.dot(chosen, projected(k), preferred_element_type=jnp.float32)
        messages[which] = sent.astype(jnp.bfloat16).reshape(toks, slots, 2 * half)
        for step in (4, 5, 3, 6, 2, 7, 1):
            delivery(which, step).start()
        kept(which).start()

    project(0)
    pass_on(0)

    @pl.loop(0, chunks)
    def _(c):
        row_x(c).wait_recv()

    project(1)
    pass_on(1)

    @pl.loop(0, chunks)
    def _(c):
        row_z(c).wait_recv()
        row_relay(c).start()

    project(2)
    pass_on(2)
    for copy in place_copies:
        copy.wait_recv()
    deliver(0)

    @pl.loop(0, chunks)
    def _(c):
        row_relay(c).wait_recv()

    project(3)
    pass_on(3)
    deliver(1)

    @pl.loop(0, chunks)
    def _(c):
        near_copy(c, 0).wait_send()
        near_copy(c, 1).wait_send()
        far_copy(c).wait_send()
        row_x(c).wait_send()
        row_z(c).wait_send()
        row_relay(c).wait_send()

    for copy in place_copies:
        copy.wait_send()
    for k in range(4):
        term_near(k, 0).wait_send()
        term_near(k, 1).wait_send()
        term_far(k).wait_send()
    for which in range(2):
        kept(which).wait()
        for step in range(1, 8):
            delivery(which, step).wait()


def block_body(
    tokens, attn_gain, qkv_weight, out_weight, merge_gain, merge_weight,
    grid_sizes, segment_ids, patch_pos, live_mask, owners,
):
    group_len = segment_ids.shape[0]
    local_rows, width = tokens.shape
    head_width = qkv_weight.shape[1]
    heads_here = head_width // HD
    tok_count = lax.axis_size("tok")
    owned = local_rows // 4
    half = merge_weight.shape[1]
    slot_count = 2 * owned // tok_count
    dma, vmem = pltpu.SemaphoreType.DMA, pltpu.VMEM

    other_weight = lax.ppermute(merge_weight, "tok", [(t, t ^ 2) for t in range(tok_count)])

    normed, residual = pl.pallas_call(
        gather_kernel,
        out_shape=(
            jax.ShapeDtypeStruct((4, 4, owned, width), jnp.bfloat16),
            jax.ShapeDtypeStruct((4, owned, width), jnp.bfloat16),
        ),
        in_specs=[VMEM_SPEC] * 2,
        out_specs=(VMEM_SPEC, VMEM_SPEC),
        scratch_shapes=[vmem((3, 4, owned, width), jnp.bfloat16)] + [dma((2, 4))] * 3,
        compiler_params=pltpu.CompilerParams(
            collective_id=0, has_side_effects=True, vmem_limit_bytes=VMEM_LIMIT
        ),
    )(tokens.reshape(owned, 4, width).transpose(1, 0, 2), attn_gain.reshape(1, width))

    def by_place(values):
        return values.reshape(values.shape[:-1] + (group_len // 4, 4)).swapaxes(-1, -2).reshape(
            values.shape
        )

    segments = by_place(segment_ids)
    key_live = by_place(live_mask) == 1
    places = by_place(patch_pos).astype(jnp.float32)
    image_count = grid_sizes.shape[1]
    local_image = segments - lax.axis_index("tok") * image_count
    image_match = local_image[:, None] == jnp.arange(image_count, dtype=jnp.int32)[None, :]
    grid_float = grid_sizes.astype(jnp.float32)
    row_size = jnp.sum(jnp.where(image_match, grid_float[0][None, :], 0.0), axis=1)
    col_size = jnp.sum(jnp.where(image_match, grid_float[1][None, :], 0.0), axis=1)
    row_coord = places[0] * SIDE / row_size
    col_coord = places[1] * SIDE / col_size
    projected_rows = lax.dot_general(
        normed.reshape(group_len, width),
        qkv_weight.reshape(3 * head_width, width),
        (((1,), (1,)), ((), ())),
        preferred_element_type=jnp.float32,
    ).reshape(group_len, 3, heads_here, HD)
    queries = (rotate(projected_rows[:, 0], row_coord, col_coord) * HD ** (-0.5)).astype(
        jnp.bfloat16
    )
    keys = rotate(projected_rows[:, 1], row_coord, col_coord).astype(jnp.bfloat16)
    values = projected_rows[:, 2].astype(jnp.bfloat16)
    order = jnp.arange(group_len, dtype=jnp.int32)
    allowed = (segments[:, None] == segments[None, :]) & (
        key_live[None, :] | (order[:, None] == order[None, :])
    )
    scores = jnp.einsum("qhd,khd->hqk", queries, keys, preferred_element_type=jnp.float32)
    masked = jnp.where(allowed[None], scores, NEGATIVE)
    row_top = jnp.max(masked, axis=2, keepdims=True)
    exponent = jnp.where(allowed[None], jnp.exp(masked - row_top), 0.0)
    denominator = jnp.sum(exponent, axis=2)
    numerator = jnp.einsum(
        "hqk,khd->qhd", exponent.astype(jnp.bfloat16), values, preferred_element_type=jnp.float32
    )
    heads_out = (numerator / denominator.T[:, :, None]).astype(jnp.bfloat16)
    part = jnp.dot(
        heads_out.reshape(group_len, head_width), out_weight, preferred_element_type=jnp.float32
    ).astype(jnp.bfloat16)

    owner_col = owners[:, 0]
    target = (owner_col * (2 * slot_count) + earlier_rows(owner_col)).astype(jnp.float32)
    target = jnp.broadcast_to(jnp.pad(target, (0, 128 - owned))[None, :], (8, 128))

    delivered = pl.pallas_call(
        merge_kernel,
        out_shape=jax.ShapeDtypeStruct((2, tok_count, 2 * slot_count, 2 * half), jnp.bfloat16),
        in_specs=[VMEM_SPEC] * 6,
        out_specs=VMEM_SPEC,
        scratch_shapes=[
            vmem((2, 4, owned, width), jnp.bfloat16),
            vmem((4, owned, width), jnp.bfloat16),
            vmem((4, owned, width), jnp.bfloat16),
            vmem((4, 4, owned, width), jnp.bfloat16),
            vmem((4, 4, owned, 2 * half), jnp.bfloat16),
            vmem((4, 2, owned, 2 * half), jnp.bfloat16),
            vmem((4, owned, 2 * half), jnp.bfloat16),
            vmem((4, owned, 2 * half), jnp.bfloat16),
            vmem((3, 8, 128), jnp.float32),
            vmem((2, tok_count, 2 * slot_count, 2 * half), jnp.bfloat16),
            dma((2, 2, 4)), dma((2, 4)), dma((2, 4)), dma((2, 4)), dma((2, 4)),
            dma((2, 4, 2)), dma((2, 4)), dma((2, 3)), dma((2, 2, tok_count)), dma((2,)),
        ],
        compiler_params=pltpu.CompilerParams(
            collective_id=1, has_side_effects=True, vmem_limit_bytes=VMEM_LIMIT
        ),
    )(
        part.reshape(4, 4, owned, width), residual, merge_gain.reshape(1, width),
        merge_weight, other_weight, target,
    )
    delivered = delivered.reshape(2, 2, 2, 2, 2, slot_count, 2, half)
    return delivered.transpose(0, 2, 4, 5, 1, 6, 3, 7).reshape(tok_count * slot_count, -1)


def solution(mesh):
    fits_blocks = mesh.shape["head"] == 4 and mesh.shape["tok"] == 8
    placed = (
        P(("tok", "head"), None),
        P(),
        P(None, "head", None),
        P("head", None),
        P(),
        P("head", "tok"),
        P(None, "tok"),
        P("tok"),
        P(None, "tok"),
        P("tok"),
        P(("tok", "head"), None),
    )
    return jax.shard_map(
        block_body if fits_blocks else body, mesh=mesh, in_specs=placed, out_specs=P(("tok", "head"), None), check_vma=False
    )
```

```python
import jax
import jax.numpy as jnp
from jax import lax
from jax.experimental import pallas as pl
from jax.experimental.pallas import tpu as pltpu
from jax.sharding import PartitionSpec as P

D = 1664
HD = 104
SIDE = 16


EPSILON = 1e-06
NEGATIVE = -1e30


def layer_norm(values, gain_vec):
    average = jnp.mean(values, axis=-1, keepdims=True)
    centred = values - average
    variance = jnp.mean(centred * centred, axis=-1, keepdims=True)
    return centred * lax.rsqrt(variance + EPSILON) * gain_vec


def rotate(vectors, row_coord, col_coord):
    quarter = vectors.shape[-1] // 4
    frequency = 10000.0 ** (-jnp.arange(quarter, dtype=jnp.float32) / quarter)
    pieces = []
    for which_axis, coordinate in ((0, row_coord), (1, col_coord)):
        leading = vectors[..., 2 * which_axis * quarter : (2 * which_axis + 1) * quarter]
        trailing = vectors[..., (2 * which_axis + 1) * quarter : (2 * which_axis + 2) * quarter]
        angles = coordinate[:, None, None] * frequency
        cosine = jnp.cos(angles)
        sine_val = jnp.sin(angles)
        pieces.append(leading * cosine - trailing * sine_val)
        pieces.append(leading * sine_val + trailing * cosine)
    return jnp.concatenate(pieces, axis=-1)


def earlier_rows(owner_col):
    places = jnp.arange(owner_col.shape[0], dtype=jnp.int32)
    same = (owner_col[:, None] == owner_col[None, :]) & (places[None, :] < places[:, None])
    return jnp.sum(same.astype(jnp.int32), axis=1, dtype=jnp.int32)


def body(
    tokens,
    attn_gain,
    qkv_weight,
    out_weight,
    merge_gain,
    merge_weight,
    grid_sizes,
    segment_ids,
    patch_pos,
    live_mask,
    owners,
):
    group_len = segment_ids.shape[0]
    local_rows = tokens.shape[0]
    head_width = qkv_weight.shape[1]
    heads_here = head_width // HD
    tok_count = lax.axis_size("tok")
    image_count = grid_sizes.shape[1]
    local_image = segment_ids - lax.axis_index("tok") * image_count
    image_match = local_image[:, None] == jnp.arange(image_count, dtype=jnp.int32)[None, :]
    grid_float = grid_sizes.astype(jnp.float32)
    row_size = jnp.sum(jnp.where(image_match, grid_float[0][None, :], 0.0), axis=1)
    col_size = jnp.sum(jnp.where(image_match, grid_float[1][None, :], 0.0), axis=1)
    row_coord = patch_pos[0].astype(jnp.float32) * SIDE / row_size
    col_coord = patch_pos[1].astype(jnp.float32) * SIDE / col_size
    stacked_weight = qkv_weight.reshape(3 * head_width, D)
    normed = layer_norm(tokens.astype(jnp.float32), attn_gain).astype(jnp.bfloat16)
    projected_rows = lax.dot_general(
        lax.all_gather(normed, "head", axis=0, tiled=True),
        stacked_weight,
        (((1,), (1,)), ((), ())),
        preferred_element_type=jnp.float32,
    )
    projected_rows = projected_rows.reshape(group_len, 3, heads_here, HD)
    query_all = (rotate(projected_rows[:, 0], row_coord, col_coord) * HD ** (-0.5)).astype(
        jnp.bfloat16
    )
    key_all = rotate(projected_rows[:, 1], row_coord, col_coord).astype(jnp.bfloat16)
    value_all = projected_rows[:, 2].astype(jnp.bfloat16)
    block_len = min(512, group_len)
    block_count = group_len // block_len
    key_live = live_mask == 1

    def allowed_pairs(query_start, span):
        query_seg = lax.dynamic_slice_in_dim(segment_ids, query_start, block_len)
        query_place = query_start + jnp.arange(block_len, dtype=jnp.int32)
        key_place = jnp.arange(span, dtype=jnp.int32)
        same_image = query_seg[:, None] == segment_ids[None, :]
        return same_image & (key_live[None, :] | (query_place[:, None] == key_place[None, :]))

    def query_block(query_start):
        queries = lax.dynamic_slice_in_dim(query_all, query_start, block_len, 0)
        allowed = allowed_pairs(query_start, group_len)
        scores = jnp.einsum("qhd,khd->hqk", queries, key_all, preferred_element_type=jnp.float32)
        masked = jnp.where(allowed[None], scores, NEGATIVE)
        row_top = jnp.max(masked, axis=2, keepdims=True)
        exponent = jnp.where(allowed[None], jnp.exp(masked - row_top), 0.0)
        denominator = jnp.sum(exponent, axis=2)
        numerator = jnp.einsum(
            "hqk,khd->qhd",
            exponent.astype(jnp.bfloat16),
            value_all,
            preferred_element_type=jnp.float32,
        )
        return (numerator / denominator.T[:, :, None]).astype(jnp.bfloat16)

    block_starts = jnp.arange(block_count, dtype=jnp.int32) * block_len
    heads_out = lax.map(query_block, block_starts).reshape(group_len, head_width)
    attn_rows = lax.psum_scatter(
        jnp.dot(heads_out, out_weight, preferred_element_type=jnp.float32).astype(jnp.bfloat16),
        "head",
        scatter_dimension=0,
        tiled=True,
    ).astype(jnp.float32)
    stream = (tokens.astype(jnp.float32) + attn_rows).reshape(local_rows // 4, 4, D)
    average = jnp.sum(stream, axis=2, keepdims=True) / D
    variance = jnp.sum(stream * stream, axis=2, keepdims=True) / D - average * average
    window_rows = ((stream - average) * lax.rsqrt(variance + EPSILON) * merge_gain).astype(
        jnp.bfloat16
    )
    merged_slice = lax.all_to_all(
        window_rows.reshape(local_rows // 4, 4 * D), "head", split_axis=1, concat_axis=0, tiled=True
    )
    merged_count = local_rows // 4
    column_terms = jnp.dot(
        merged_slice,
        lax.all_gather(merge_weight, "tok", axis=1, tiled=True),
        preferred_element_type=jnp.float32,
    )
    projected = lax.psum_scatter(
        column_terms.astype(jnp.bfloat16), "head", scatter_dimension=0, tiled=True
    )
    slot_count = max(2, 2 * merged_count // tok_count)
    owner_col = owners[:, 0]
    slot_index = earlier_rows(owner_col)
    target = owner_col * slot_count + slot_index
    select = (
        jnp.arange(tok_count * slot_count, dtype=jnp.int32)[:, None] == target[None, :]
    ).astype(jnp.bfloat16)
    send_rows = jnp.dot(select, projected, preferred_element_type=jnp.float32).astype(jnp.bfloat16)
    send_rows = send_rows.reshape(tok_count, slot_count, -1)
    received = lax.all_to_all(send_rows, "tok", split_axis=0, concat_axis=0, tiled=True)
    return received.reshape(tok_count * slot_count, -1)


VMEM_SPEC = pl.BlockSpec(memory_space=pltpu.VMEM)
MESH = pl.DeviceIdType.MESH
VMEM_LIMIT = 48 * 1024 * 1024


def remote(source, target, send, arrive, tok, head):
    return pltpu.make_async_remote_copy(
        src_ref=source,
        dst_ref=target,
        send_sem=send,
        recv_sem=arrive,
        device_id=(tok, head),
        device_id_type=MESH,
    )


def greet(devices):
    barrier = pltpu.get_barrier_semaphore()
    for device in devices:
        pl.semaphore_signal(barrier, inc=1, device_id=device, device_id_type=MESH)
    pl.semaphore_wait(barrier, len(devices))


def head_partners():
    tok, head = lax.axis_index("tok"), lax.axis_index("head")
    sibling = head + 1 - 2 * (head % 2)
    across = (head + 2) % 4
    return tok, head, sibling, across


def gather_kernel(
    tokens_ref, gain_ref, normed_ref, residual_ref, raw, own_sems, across_sems, relay_sems
):
    tok, head, sibling, across = head_partners()
    diagonal = (sibling + 2) % 4
    parts = tokens_ref.shape[0]
    greet([(tok, sibling), (tok, across)])

    def to_across(r):
        return remote(
            tokens_ref.at[r], raw.at[1, r], across_sems.at[0, r], across_sems.at[1, r], tok, across
        )

    def to_sibling(r):
        return remote(
            tokens_ref.at[r], raw.at[0, r], own_sems.at[0, r], own_sems.at[1, r], tok, sibling
        )

    def relay(r):
        return remote(
            raw.at[1, r], raw.at[2, r], relay_sems.at[0, r], relay_sems.at[1, r], tok, sibling
        )

    def settle(rows, r, source):
        values = rows.astype(jnp.float32)
        average = jnp.mean(values, axis=-1, keepdims=True)
        centred = values - average
        variance = jnp.mean(centred * centred, axis=-1, keepdims=True)
        normal = centred * lax.rsqrt(variance + EPSILON) * gain_ref[...][None, :]
        normed_ref[r, source] = normal.astype(jnp.bfloat16)

    for r in range(parts):
        to_across(r).start()
    for r in range(parts):
        to_sibling(r).start()

    @pl.loop(0, parts)
    def _(r):
        settle(tokens_ref[r], r, head)

    @pl.loop(0, parts)
    def _(r):
        to_sibling(r).wait_recv()
        settle(raw[0, r], r, sibling)

    @pl.loop(0, parts)
    def _(r):
        to_across(r).wait_recv()
        relay(r).start()
        settle(raw[1, r], r, across)

    @pl.loop(0, parts)
    def _(r):
        relay(r).wait_recv()
        settle(raw[2, r], r, diagonal)

    residual_ref[head] = tokens_ref[head]
    residual_ref[sibling] = raw[0, head]
    residual_ref[across] = raw[1, head]
    residual_ref[diagonal] = raw[2, head]

    @pl.loop(0, parts)
    def _(r):
        to_across(r).wait_send()
        to_sibling(r).wait_send()
        relay(r).wait_send()


def merge_kernel(
    part_ref, residual_ref, gain_ref, weight_ref, other_ref, target_ref, out_ref,
    near_sum, sent_sum, far_sum, rows, terms, near_term, sent_term, far_term, places, messages,
    sum_near_sems, sum_far_sems, row_x_sems, row_z_sems, row_relay_sems,
    term_near_sems, term_far_sems, place_sems, out_sems, local_sems,
):
    tok, head, sibling, across = head_partners()
    diagonal = (sibling + 2) % 4
    toks = lax.axis_size("tok")
    p, q, x = tok // 4, (tok // 2) % 2, tok % 2
    beside = tok + 1 - 2 * x
    over = (tok + 4) % 8
    corner = (beside + 4) % 8
    span = near_sum.shape[2]
    chunks = part_ref.shape[1]
    owned = near_term.shape[2]
    half = weight_ref.shape[1]
    greet(
        [((tok + step) % toks, head) for step in range(1, toks)] + [(tok, sibling), (tok, across)]
    )

    def near_copy(c, which):
        block = (diagonal, sibling)[which]
        return remote(
            part_ref.at[block, c], near_sum.at[which, c],
            sum_near_sems.at[0, which, c], sum_near_sems.at[1, which, c], tok, sibling,
        )

    def far_copy(c):
        return remote(
            sent_sum.at[c], far_sum.at[c], sum_far_sems.at[0, c], sum_far_sems.at[1, c], tok, across
        )

    order = (diagonal, sibling, across, head)
    for c in order:
        near_copy(c, 0).start()
    for c in order:
        near_copy(c, 1).start()
    place_copies = [
        remote(
            target_ref, places.at[k], place_sems.at[0, k], place_sems.at[1, k], device, head
        )
        for k, device in enumerate((beside, over, corner))
    ]
    for copy in place_copies:
        copy.start()

    for c in order:
        near_copy(c, 0).wait_recv()
        total = part_ref[across, c].astype(jnp.float32) + near_sum[0, c].astype(jnp.float32)
        sent_sum[c] = total.astype(jnp.bfloat16)
        far_copy(c).start()

    def row_x(c):
        return remote(
            rows.at[0, c], rows.at[1, c], row_x_sems.at[0, c], row_x_sems.at[1, c], beside, head
        )

    def row_z(c):
        return remote(
            rows.at[0, c], rows.at[2, c], row_z_sems.at[0, c], row_z_sems.at[1, c], over, head
        )

    def row_relay(c):
        return remote(
            rows.at[2, c], rows.at[3, c],
            row_relay_sems.at[0, c], row_relay_sems.at[1, c], beside, head,
        )

    width = residual_ref.shape[-1]

    for c in order:
        near_copy(c, 1).wait_recv()
        stream = residual_ref[c].astype(jnp.float32) + part_ref[head, c].astype(jnp.float32)
        stream = stream + near_sum[1, c].astype(jnp.float32)
        far_copy(c).wait_recv()
        stream = stream + far_sum[c].astype(jnp.float32)
        average = jnp.sum(stream, axis=-1, keepdims=True) / width
        variance = jnp.sum(stream * stream, axis=-1, keepdims=True) / width - average * average
        normal = (stream - average) * lax.rsqrt(variance + EPSILON) * gain_ref[...][None, :]
        rows[0, c] = normal.astype(jnp.bfloat16)
        row_z(c).start()
        row_x(c).start()

    own_columns = pl.ds(pl.multiple_of(q * half, half), half)
    other_columns = pl.ds(pl.multiple_of((1 - q) * half, half), half)

    def term_near(k, which):
        block = (diagonal, sibling)[which]
        return remote(
            terms.at[k, block], near_term.at[k, which],
            term_near_sems.at[0, k, which], term_near_sems.at[1, k, which], tok, sibling,
        )

    def term_far(k):
        return remote(
            sent_term.at[k], far_term.at[k], term_far_sems.at[0, k], term_far_sems.at[1, k],
            tok, across,
        )

    def project(k, members):
        block = jnp.concatenate([rows[k, c] for c in members], axis=0)
        for weights, columns in ((weight_ref, own_columns), (other_ref, other_columns)):
            product = jnp.dot(block, weights[...], preferred_element_type=jnp.float32)
            product = product.astype(jnp.bfloat16)
            for turn, c in enumerate(members):
                terms[k, c, :, columns] = product[turn * span : (turn + 1) * span]
        if diagonal is members[0]:
            term_near(k, 0).start()
            term_near(k, 1).start()

    def pass_on(k):
        term_near(k, 0).wait_recv()
        total = terms[k, across].astype(jnp.float32) + near_term[k, 0].astype(jnp.float32)
        sent_term[k] = total.astype(jnp.bfloat16)
        term_far(k).start()

    def projected(k):
        term_near(k, 1).wait_recv()
        total = terms[k, head].astype(jnp.float32) + near_term[k, 1].astype(jnp.float32)
        term_far(k).wait_recv()
        return (total + far_term[k].astype(jnp.float32)).astype(jnp.bfloat16)

    slots = messages.shape[2]

    def delivery(which, step):
        owner = (tok + step) % toks
        group = p if which == 0 else 1 - p
        return remote(
            messages.at[which, owner], out_ref.at[group, tok],
            out_sems.at[0, which, step], out_sems.at[1, which, step], owner, head,
        )

    def kept(which):
        group = p if which == 0 else 1 - p
        return pltpu.make_async_copy(
            messages.at[which, tok], out_ref.at[group, tok], local_sems.at[which]
        )

    def deliver(which):
        lines = lax.broadcasted_iota(jnp.int32, (toks * slots, owned), 0).astype(jnp.float32)
        sent = jnp.zeros((toks * slots, 2 * half), jnp.float32)
        for turn in range(2):
            k = 2 * which + turn
            aim = target_ref[0:1, 0:owned] if k == 0 else places[k - 1, 0:1, 0:owned]
            side = x if turn == 0 else 1 - x
            aim = aim + (side * (slots // 2)).astype(jnp.float32)
            chosen = jnp.where(lines == aim, 1.0, 0.0).astype(jnp.bfloat16)
            sent = sent + jnp.dot(chosen, projected(k), preferred_element_type=jnp.float32)
        messages[which] = sent.astype(jnp.bfloat16).reshape(toks, slots, 2 * half)
        for step in (4, 5, 3, 6, 2, 7, 1):
            delivery(which, step).start()
        kept(which).start()

    project(0, order)
    pass_on(0)
    for c in order:
        row_x(c).wait_recv()
    project(1, order)
    pass_on(1)
    for copy in place_copies:
        copy.wait_recv()
    for c in order:
        row_z(c).wait_recv()
        row_relay(c).start()
    deliver(0)
    project(2, order)
    for pair in (order[:2], order[2:]):
        for c in pair:
            row_relay(c).wait_recv()
        project(3, pair)
        if pair[0] is diagonal:
            pass_on(2)
    pass_on(3)
    deliver(1)

    @pl.loop(0, chunks)
    def _(c):
        near_copy(c, 0).wait_send()
        near_copy(c, 1).wait_send()
        far_copy(c).wait_send()
        row_x(c).wait_send()
        row_z(c).wait_send()
        row_relay(c).wait_send()

    for copy in place_copies:
        copy.wait_send()
    for k in range(4):
        term_near(k, 0).wait_send()
        term_near(k, 1).wait_send()
        term_far(k).wait_send()
    for which in range(2):
        kept(which).wait()
        for step in range(1, 8):
            delivery(which, step).wait()


def block_body(
    tokens, attn_gain, qkv_weight, out_weight, merge_gain, merge_weight,
    grid_sizes, segment_ids, patch_pos, live_mask, owners,
):
    group_len = segment_ids.shape[0]
    local_rows, width = tokens.shape
    head_width = qkv_weight.shape[1]
    heads_here = head_width // HD
    tok_count = lax.axis_size("tok")
    owned = local_rows // 4
    half = merge_weight.shape[1]
    slot_count = 2 * owned // tok_count
    dma, vmem = pltpu.SemaphoreType.DMA, pltpu.VMEM

    other_weight = lax.ppermute(merge_weight, "tok", [(t, t ^ 2) for t in range(tok_count)])

    normed, residual = pl.pallas_call(
        gather_kernel,
        out_shape=(
            jax.ShapeDtypeStruct((4, 4, owned, width), jnp.bfloat16),
            jax.ShapeDtypeStruct((4, owned, width), jnp.bfloat16),
        ),
        in_specs=[VMEM_SPEC] * 2,
        out_specs=(VMEM_SPEC, VMEM_SPEC),
        scratch_shapes=[vmem((3, 4, owned, width), jnp.bfloat16)] + [dma((2, 4))] * 3,
        compiler_params=pltpu.CompilerParams(
            collective_id=0, has_side_effects=True, vmem_limit_bytes=VMEM_LIMIT
        ),
    )(tokens.reshape(owned, 4, width).transpose(1, 0, 2), attn_gain)

    def by_place(values):
        return values.reshape(values.shape[:-1] + (group_len // 4, 4)).swapaxes(-1, -2).reshape(
            values.shape
        )

    segments = by_place(segment_ids)
    key_live = by_place(live_mask) == 1
    places = by_place(patch_pos).astype(jnp.float32)
    image_count = grid_sizes.shape[1]
    local_image = segments - lax.axis_index("tok") * image_count
    image_match = local_image[:, None] == jnp.arange(image_count, dtype=jnp.int32)[None, :]
    grid_float = grid_sizes.astype(jnp.float32)
    row_size = jnp.sum(jnp.where(image_match, grid_float[0][None, :], 0.0), axis=1)
    col_size = jnp.sum(jnp.where(image_match, grid_float[1][None, :], 0.0), axis=1)
    row_coord = places[0] * SIDE / row_size
    col_coord = places[1] * SIDE / col_size
    projected_rows = lax.dot_general(
        normed.reshape(group_len, width),
        qkv_weight.reshape(3 * head_width, width),
        (((1,), (1,)), ((), ())),
        preferred_element_type=jnp.float32,
    ).reshape(group_len, 3, heads_here, HD)
    queries = (rotate(projected_rows[:, 0], row_coord, col_coord) * HD ** (-0.5)).astype(
        jnp.bfloat16
    )
    keys = rotate(projected_rows[:, 1], row_coord, col_coord).astype(jnp.bfloat16)
    values = projected_rows[:, 2].astype(jnp.bfloat16)
    order = jnp.arange(group_len, dtype=jnp.int32)
    allowed = (segments[:, None] == segments[None, :]) & (
        key_live[None, :] | (order[:, None] == order[None, :])
    )
    scores = jnp.einsum("qhd,khd->hqk", queries, keys, preferred_element_type=jnp.float32)
    masked = jnp.where(allowed[None], scores, NEGATIVE)
    row_top = jnp.max(masked, axis=2, keepdims=True)
    exponent = jnp.where(allowed[None], jnp.exp(masked - row_top), 0.0)
    denominator = jnp.sum(exponent, axis=2)
    numerator = jnp.einsum(
        "hqk,khd->qhd", exponent.astype(jnp.bfloat16), values, preferred_element_type=jnp.float32
    )
    heads_out = (numerator / denominator.T[:, :, None]).astype(jnp.bfloat16)
    part = jnp.dot(
        heads_out.reshape(group_len, head_width), out_weight, preferred_element_type=jnp.float32
    ).astype(jnp.bfloat16)

    owner_col = owners[:, 0]
    target = (owner_col * (2 * slot_count) + earlier_rows(owner_col)).astype(jnp.float32)
    target = jnp.broadcast_to(jnp.pad(target, (0, 128 - owned))[None, :], (8, 128))

    delivered = pl.pallas_call(
        merge_kernel,
        out_shape=jax.ShapeDtypeStruct((2, tok_count, 2 * slot_count, 2 * half), jnp.bfloat16),
        in_specs=[VMEM_SPEC] * 6,
        out_specs=VMEM_SPEC,
        scratch_shapes=[
            vmem((2, 4, owned, width), jnp.bfloat16),
            vmem((4, owned, width), jnp.bfloat16),
            vmem((4, owned, width), jnp.bfloat16),
            vmem((4, 4, owned, width), jnp.bfloat16),
            vmem((4, 4, owned, 2 * half), jnp.bfloat16),
            vmem((4, 2, owned, 2 * half), jnp.bfloat16),
            vmem((4, owned, 2 * half), jnp.bfloat16),
            vmem((4, owned, 2 * half), jnp.bfloat16),
            vmem((3, 8, 128), jnp.float32),
            vmem((2, tok_count, 2 * slot_count, 2 * half), jnp.bfloat16),
            dma((2, 2, 4)), dma((2, 4)), dma((2, 4)), dma((2, 4)), dma((2, 4)),
            dma((2, 4, 2)), dma((2, 4)), dma((2, 3)), dma((2, 2, tok_count)), dma((2,)),
        ],
        compiler_params=pltpu.CompilerParams(
            collective_id=1, has_side_effects=True, vmem_limit_bytes=VMEM_LIMIT
        ),
    )(
        part.reshape(4, 4, owned, width), residual, merge_gain,
        merge_weight, other_weight, target,
    )
    delivered = delivered.reshape(2, 2, 2, 2, 2, slot_count, 2, half)
    return delivered.transpose(0, 2, 4, 5, 1, 6, 3, 7).reshape(tok_count * slot_count, -1)


def solution(mesh):
    fits_blocks = mesh.shape["head"] == 4 and mesh.shape["tok"] == 8
    placed = (
        P(("tok", "head"), None),
        P(),
        P(None, "head", None),
        P("head", None),
        P(),
        P("head", "tok"),
        P(None, "tok"),
        P("tok"),
        P(None, "tok"),
        P("tok"),
        P(("tok", "head"), None),
    )
    return jax.shard_map(
        block_body if fits_blocks else body, mesh=mesh, in_specs=placed, out_specs=P(("tok", "head"), None), check_vma=False
    )
```

```python
import jax
import jax.numpy as jnp
from jax import lax
from jax.experimental import pallas as pl
from jax.experimental.pallas import tpu as pltpu
from jax.sharding import PartitionSpec as P

D = 1664
HD = 104
SIDE = 16


EPSILON = 1e-06
NEGATIVE = -1e30


def layer_norm(values, gain_vec):
    average = jnp.mean(values, axis=-1, keepdims=True)
    centred = values - average
    variance = jnp.mean(centred * centred, axis=-1, keepdims=True)
    return centred * lax.rsqrt(variance + EPSILON) * gain_vec


def rotate(vectors, row_coord, col_coord):
    quarter = vectors.shape[-1] // 4
    frequency = 10000.0 ** (-jnp.arange(quarter, dtype=jnp.float32) / quarter)
    pieces = []
    for which_axis, coordinate in ((0, row_coord), (1, col_coord)):
        leading = vectors[..., 2 * which_axis * quarter : (2 * which_axis + 1) * quarter]
        trailing = vectors[..., (2 * which_axis + 1) * quarter : (2 * which_axis + 2) * quarter]
        angles = coordinate[:, None, None] * frequency
        cosine = jnp.cos(angles)
        sine_val = jnp.sin(angles)
        pieces.append(leading * cosine - trailing * sine_val)
        pieces.append(leading * sine_val + trailing * cosine)
    return jnp.concatenate(pieces, axis=-1)


def earlier_rows(owner_col):
    places = jnp.arange(owner_col.shape[0], dtype=jnp.int32)
    same = (owner_col[:, None] == owner_col[None, :]) & (places[None, :] < places[:, None])
    return jnp.sum(same.astype(jnp.int32), axis=1, dtype=jnp.int32)


def body(
    tokens,
    attn_gain,
    qkv_weight,
    out_weight,
    merge_gain,
    merge_weight,
    grid_sizes,
    segment_ids,
    patch_pos,
    live_mask,
    owners,
):
    group_len = segment_ids.shape[0]
    local_rows = tokens.shape[0]
    head_width = qkv_weight.shape[1]
    heads_here = head_width // HD
    tok_count = lax.axis_size("tok")
    image_count = grid_sizes.shape[1]
    local_image = segment_ids - lax.axis_index("tok") * image_count
    image_match = local_image[:, None] == jnp.arange(image_count, dtype=jnp.int32)[None, :]
    grid_float = grid_sizes.astype(jnp.float32)
    row_size = jnp.sum(jnp.where(image_match, grid_float[0][None, :], 0.0), axis=1)
    col_size = jnp.sum(jnp.where(image_match, grid_float[1][None, :], 0.0), axis=1)
    row_coord = patch_pos[0].astype(jnp.float32) * SIDE / row_size
    col_coord = patch_pos[1].astype(jnp.float32) * SIDE / col_size
    stacked_weight = qkv_weight.reshape(3 * head_width, D)
    normed = layer_norm(tokens.astype(jnp.float32), attn_gain).astype(jnp.bfloat16)
    projected_rows = lax.dot_general(
        lax.all_gather(normed, "head", axis=0, tiled=True),
        stacked_weight,
        (((1,), (1,)), ((), ())),
        preferred_element_type=jnp.float32,
    )
    projected_rows = projected_rows.reshape(group_len, 3, heads_here, HD)
    query_all = (rotate(projected_rows[:, 0], row_coord, col_coord) * HD ** (-0.5)).astype(
        jnp.bfloat16
    )
    key_all = rotate(projected_rows[:, 1], row_coord, col_coord).astype(jnp.bfloat16)
    value_all = projected_rows[:, 2].astype(jnp.bfloat16)
    block_len = min(512, group_len)
    block_count = group_len // block_len
    key_live = live_mask == 1

    def allowed_pairs(query_start, span):
        query_seg = lax.dynamic_slice_in_dim(segment_ids, query_start, block_len)
        query_place = query_start + jnp.arange(block_len, dtype=jnp.int32)
        key_place = jnp.arange(span, dtype=jnp.int32)
        same_image = query_seg[:, None] == segment_ids[None, :]
        return same_image & (key_live[None, :] | (query_place[:, None] == key_place[None, :]))

    def query_block(query_start):
        queries = lax.dynamic_slice_in_dim(query_all, query_start, block_len, 0)
        allowed = allowed_pairs(query_start, group_len)
        scores = jnp.einsum("qhd,khd->hqk", queries, key_all, preferred_element_type=jnp.float32)
        masked = jnp.where(allowed[None], scores, NEGATIVE)
        row_top = jnp.max(masked, axis=2, keepdims=True)
        exponent = jnp.where(allowed[None], jnp.exp(masked - row_top), 0.0)
        denominator = jnp.sum(exponent, axis=2)
        numerator = jnp.einsum(
            "hqk,khd->qhd",
            exponent.astype(jnp.bfloat16),
            value_all,
            preferred_element_type=jnp.float32,
        )
        return (numerator / denominator.T[:, :, None]).astype(jnp.bfloat16)

    block_starts = jnp.arange(block_count, dtype=jnp.int32) * block_len
    heads_out = lax.map(query_block, block_starts).reshape(group_len, head_width)
    attn_rows = lax.psum_scatter(
        jnp.dot(heads_out, out_weight, preferred_element_type=jnp.float32).astype(jnp.bfloat16),
        "head",
        scatter_dimension=0,
        tiled=True,
    ).astype(jnp.float32)
    stream = (tokens.astype(jnp.float32) + attn_rows).reshape(local_rows // 4, 4, D)
    average = jnp.sum(stream, axis=2, keepdims=True) / D
    variance = jnp.sum(stream * stream, axis=2, keepdims=True) / D - average * average
    window_rows = ((stream - average) * lax.rsqrt(variance + EPSILON) * merge_gain).astype(
        jnp.bfloat16
    )
    merged_slice = lax.all_to_all(
        window_rows.reshape(local_rows // 4, 4 * D), "head", split_axis=1, concat_axis=0, tiled=True
    )
    merged_count = local_rows // 4
    column_terms = jnp.dot(
        merged_slice,
        lax.all_gather(merge_weight, "tok", axis=1, tiled=True),
        preferred_element_type=jnp.float32,
    )
    projected = lax.psum_scatter(
        column_terms.astype(jnp.bfloat16), "head", scatter_dimension=0, tiled=True
    )
    slot_count = max(2, 2 * merged_count // tok_count)
    owner_col = owners[:, 0]
    slot_index = earlier_rows(owner_col)
    target = owner_col * slot_count + slot_index
    select = (
        jnp.arange(tok_count * slot_count, dtype=jnp.int32)[:, None] == target[None, :]
    ).astype(jnp.bfloat16)
    send_rows = jnp.dot(select, projected, preferred_element_type=jnp.float32).astype(jnp.bfloat16)
    send_rows = send_rows.reshape(tok_count, slot_count, -1)
    received = lax.all_to_all(send_rows, "tok", split_axis=0, concat_axis=0, tiled=True)
    return received.reshape(tok_count * slot_count, -1)


VMEM_SPEC = pl.BlockSpec(memory_space=pltpu.VMEM)
MESH = pl.DeviceIdType.MESH
VMEM_LIMIT = 48 * 1024 * 1024


def remote(source, target, send, arrive, tok, head):
    return pltpu.make_async_remote_copy(
        src_ref=source,
        dst_ref=target,
        send_sem=send,
        recv_sem=arrive,
        device_id=(tok, head),
        device_id_type=MESH,
    )


def greet(devices):
    barrier = pltpu.get_barrier_semaphore()
    for device in devices:
        pl.semaphore_signal(barrier, inc=1, device_id=device, device_id_type=MESH)
    pl.semaphore_wait(barrier, len(devices))


def head_partners():
    tok, head = lax.axis_index("tok"), lax.axis_index("head")
    sibling = head + 1 - 2 * (head % 2)
    across = (head + 2) % 4
    return tok, head, sibling, across


def layer_kernel(
    tokens_ref, attn_gain_ref, gain_ref, turns_ref, lanes_ref, columns_ref, target_ref,
    qkv_hbm, out_hbm, merge_hbm, out_ref,
    qkv_ref, outw_ref, weight_ref, other_ref, raw, normed, residual_ref, queries, keys, held, tables, part_ref,
    near_sum, sent_sum, far_sum, rows, terms, near_term, sent_term, far_term, places, messages,
    load_sems, weight_sems, own_sems, across_sems, relay_sems,
    sum_near_sems, sum_far_sems, row_x_sems, row_z_sems, row_relay_sems,
    term_near_sems, term_far_sems, place_sems, out_sems, local_sems,
):
    tok, head, sibling, across = head_partners()
    diagonal = (sibling + 2) % 4
    toks = lax.axis_size("tok")
    p, q, x = tok // 4, (tok // 2) % 2, tok % 2
    beside = tok + 1 - 2 * x
    paired = tok + 2 - 4 * q
    over = (tok + 4) % 8
    corner = (beside + 4) % 8
    span = near_sum.shape[2]
    chunks = part_ref.shape[1]
    owned = near_term.shape[2]
    half = weight_ref.shape[1]
    width = residual_ref.shape[-1]
    local = chunks * span
    loads = [
        pltpu.make_async_copy(source, target, load_sems.at[i])
        for i, (source, target) in enumerate(
            ((qkv_hbm, qkv_ref), (out_hbm, outw_ref), (merge_hbm, weight_ref))
        )
    ]
    for load in loads:
        load.start()
    greet(
        [((tok + step) % toks, head) for step in range(1, toks)] + [(tok, sibling), (tok, across)]
    )

    def to_across(r):
        return remote(
            tokens_ref.at[r], raw.at[1, r], across_sems.at[0, r], across_sems.at[1, r], tok, across
        )

    def to_sibling(r):
        return remote(
            tokens_ref.at[r], raw.at[0, r], own_sems.at[0, r], own_sems.at[1, r], tok, sibling
        )

    def relay(r):
        return remote(
            raw.at[1, r], raw.at[2, r], relay_sems.at[0, r], relay_sems.at[1, r], tok, sibling
        )

    for r in range(chunks):
        to_across(r).start()
    for r in range(chunks):
        to_sibling(r).start()
    weight_copy = remote(merge_hbm, other_ref, weight_sems.at[0], weight_sems.at[1], paired, head)
    weight_copy.start()
    place_copies = [
        remote(
            target_ref, places.at[k], place_sems.at[0, k], place_sems.at[1, k], device, head
        )
        for k, device in enumerate((beside, over, corner))
    ]
    for copy in place_copies:
        copy.start()

    heads_here = queries.shape[0]
    angles = jnp.where(turns_ref[:, 1:2] == 0.0, lanes_ref[0:1, :], lanes_ref[1:2, :])
    angles = angles * turns_ref[:, 0:1]
    cosine = jnp.cos(angles)
    sine = jnp.sin(angles) * turns_ref[:, 2:3]
    tables[0] = cosine
    tables[1] = sine
    row_places = lax.broadcasted_iota(jnp.int32, (span, local), 0)
    token_places = lax.broadcasted_iota(jnp.int32, (span, local), 1)
    own_rows = jnp.where(token_places == 4 * row_places + head, 1.0, 0.0).astype(jnp.bfloat16)
    spread = lax.broadcasted_iota(jnp.int32, (local, local), 0)
    spread = 4 * (spread % span) + spread // span
    by_place = jnp.where(
        lax.broadcasted_iota(jnp.int32, (local, local), 1) == spread, 1.0, 0.0
    ).astype(jnp.bfloat16)

    def settle(piece, r):
        values = piece.astype(jnp.float32)
        average = jnp.mean(values, axis=-1, keepdims=True)
        centred = values - average
        variance = jnp.mean(centred * centred, axis=-1, keepdims=True)
        normal = centred * lax.rsqrt(variance + EPSILON) * attn_gain_ref[...][None, :]
        normed[r] = normal.astype(jnp.bfloat16)

    def spin(values, lanes, factor):
        quarter = HD // 4
        a, b, c, d = (values[i * quarter : (i + 1) * quarter] for i in range(4))
        swapped = jnp.concatenate([b, a, d, c], axis=0)
        return (values * tables[0, :, lanes] + swapped * tables[1, :, lanes]) * factor

    def take_in(source, whole):
        residual_ref[source] = jnp.dot(
            own_rows, whole, preferred_element_type=jnp.float32
        ).astype(jnp.bfloat16)
        lanes = pl.ds(pl.multiple_of(source * local, local), local)
        block = normed[...].reshape(local, width)
        for which in range(3):
            product = lax.dot_general(
                qkv_ref[which], block, (((1,), (1,)), ((), ())), preferred_element_type=jnp.float32
            )
            for n in range(heads_here):
                values = product[n * HD : (n + 1) * HD]
                if which == 0:
                    queries[n, :, lanes] = spin(values, lanes, HD ** (-0.5)).astype(jnp.bfloat16)
                elif which == 1:
                    keys[n, lanes, :] = spin(values, lanes, 1.0).T.astype(jnp.bfloat16)
                else:
                    held[n, :, lanes] = values.astype(jnp.bfloat16)

    for r in range(chunks):
        settle(tokens_ref[r], r)
    loads[0].wait()
    take_in(head, tokens_ref[...].reshape(local, width))
    for r in range(chunks):
        to_sibling(r).wait_recv()
        settle(raw[0, r], r)
    take_in(sibling, raw[0].reshape(local, width))
    for r in range(chunks):
        to_across(r).wait_recv()
        relay(r).start()
        settle(raw[1, r], r)
    take_in(across, raw[1].reshape(local, width))
    for r in range(chunks):
        relay(r).wait_recv()
        settle(raw[2, r], r)
    take_in(diagonal, raw[2].reshape(local, width))
    loads[1].wait()

    def attend(c):
        lanes = pl.ds(pl.multiple_of(c * local, local), local)
        group = columns_ref.shape[0]
        key_places = lax.broadcasted_iota(jnp.int32, (group, local), 0)
        query_places = lax.broadcasted_iota(jnp.int32, (group, local), 1) + c * local
        allowed = (columns_ref[:, 0:1] == lanes_ref[2:3, lanes]) & (
            (columns_ref[:, 1:2] == 1.0) | (key_places == query_places)
        )
        pieces = []
        for n in range(heads_here):
            scores = jnp.dot(keys[n], queries[n, :, lanes], preferred_element_type=jnp.float32)
            masked = jnp.where(allowed, scores, NEGATIVE)
            top = jnp.max(masked, axis=0, keepdims=True)
            exponent = jnp.where(allowed, jnp.exp(masked - top), 0.0)
            total = jnp.sum(exponent, axis=0, keepdims=True)
            numerator = jnp.dot(
                held[n], exponent.astype(jnp.bfloat16), preferred_element_type=jnp.float32
            )
            pieces.append(numerator / total)
        heads_out = jnp.concatenate(pieces, axis=0).astype(jnp.bfloat16)
        ordered = lax.dot_general(
            by_place, heads_out, (((1,), (1,)), ((), ())), preferred_element_type=jnp.float32
        ).astype(jnp.bfloat16)
        part = jnp.dot(ordered, outw_ref[...], preferred_element_type=jnp.float32)
        part = part.astype(jnp.bfloat16)
        for r in range(4):
            part_ref[r, c] = part[r * span : (r + 1) * span]

    def near_copy(c, which):
        block = (diagonal, sibling)[which]
        return remote(
            part_ref.at[block, c], near_sum.at[which, c],
            sum_near_sems.at[0, which, c], sum_near_sems.at[1, which, c], tok, sibling,
        )

    def far_copy(c):
        return remote(
            sent_sum.at[c], far_sum.at[c], sum_far_sems.at[0, c], sum_far_sems.at[1, c], tok, across
        )

    order = (0, 1, 2, 3)

    def row_x(c):
        return remote(
            rows.at[0, c], rows.at[1, c], row_x_sems.at[0, c], row_x_sems.at[1, c], beside, head
        )

    def row_z(c):
        return remote(
            rows.at[0, c], rows.at[2, c], row_z_sems.at[0, c], row_z_sems.at[1, c], over, head
        )

    def row_relay(c):
        return remote(
            rows.at[2, c], rows.at[3, c],
            row_relay_sems.at[0, c], row_relay_sems.at[1, c], beside, head,
        )

    def pair_sum(c):
        near_copy(c, 0).wait_recv()
        total = part_ref[across, c].astype(jnp.float32) + near_sum[0, c].astype(jnp.float32)
        sent_sum[c] = total.astype(jnp.bfloat16)
        far_copy(c).start()

    def merge_rows(c):
        near_copy(c, 1).wait_recv()
        stream = residual_ref[c].astype(jnp.float32) + part_ref[head, c].astype(jnp.float32)
        stream = stream + near_sum[1, c].astype(jnp.float32)
        far_copy(c).wait_recv()
        stream = stream + far_sum[c].astype(jnp.float32)
        average = jnp.sum(stream, axis=-1, keepdims=True) / width
        variance = jnp.sum(stream * stream, axis=-1, keepdims=True) / width - average * average
        normal = (stream - average) * lax.rsqrt(variance + EPSILON) * gain_ref[...][None, :]
        rows[0, c] = normal.astype(jnp.bfloat16)
        row_z(c).start()
        row_x(c).start()

    for turn, c in enumerate(order):
        attend(c)
        near_copy(c, 0).start()
        near_copy(c, 1).start()
        if turn >= 1:
            pair_sum(order[turn - 1])
        if turn >= 2:
            merge_rows(order[turn - 2])
    pair_sum(order[-1])
    merge_rows(order[-2])
    merge_rows(order[-1])

    own_columns = pl.ds(pl.multiple_of(q * half, half), half)
    other_columns = pl.ds(pl.multiple_of((1 - q) * half, half), half)

    def term_near(k, which):
        block = (diagonal, sibling)[which]
        return remote(
            terms.at[k, block], near_term.at[k, which],
            term_near_sems.at[0, k, which], term_near_sems.at[1, k, which], tok, sibling,
        )

    def term_far(k):
        return remote(
            sent_term.at[k], far_term.at[k], term_far_sems.at[0, k], term_far_sems.at[1, k],
            tok, across,
        )

    def project(k, members):
        block = jnp.concatenate([rows[k, c] for c in members], axis=0)
        for weights, columns in ((weight_ref, own_columns), (other_ref, other_columns)):
            product = jnp.dot(block, weights[...], preferred_element_type=jnp.float32)
            product = product.astype(jnp.bfloat16)
            for turn, c in enumerate(members):
                terms[k, c, :, columns] = product[turn * span : (turn + 1) * span]
        if members[-1] == order[-1]:
            term_near(k, 0).start()
            term_near(k, 1).start()

    def pass_on(k):
        term_near(k, 0).wait_recv()
        total = terms[k, across].astype(jnp.float32) + near_term[k, 0].astype(jnp.float32)
        sent_term[k] = total.astype(jnp.bfloat16)
        term_far(k).start()

    def projected(k):
        term_near(k, 1).wait_recv()
        total = terms[k, head].astype(jnp.float32) + near_term[k, 1].astype(jnp.float32)
        term_far(k).wait_recv()
        return (total + far_term[k].astype(jnp.float32)).astype(jnp.bfloat16)

    slots = messages.shape[2]

    def delivery(which, step):
        owner = (tok + step) % toks
        group = p if which == 0 else 1 - p
        return remote(
            messages.at[which, owner], out_ref.at[group, tok],
            out_sems.at[0, which, step], out_sems.at[1, which, step], owner, head,
        )

    def kept(which):
        group = p if which == 0 else 1 - p
        return pltpu.make_async_copy(
            messages.at[which, tok], out_ref.at[group, tok], local_sems.at[which]
        )

    def deliver(which):
        lines = lax.broadcasted_iota(jnp.int32, (toks * slots, owned), 0).astype(jnp.float32)
        sent = jnp.zeros((toks * slots, 2 * half), jnp.float32)
        for turn in range(2):
            k = 2 * which + turn
            aim = target_ref[0:1, 0:owned] if k == 0 else places[k - 1, 0:1, 0:owned]
            side = x if turn == 0 else 1 - x
            aim = aim + (side * (slots // 2)).astype(jnp.float32)
            chosen = jnp.where(lines == aim, 1.0, 0.0).astype(jnp.bfloat16)
            sent = sent + jnp.dot(chosen, projected(k), preferred_element_type=jnp.float32)
        messages[which] = sent.astype(jnp.bfloat16).reshape(toks, slots, 2 * half)
        for step in (4, 5, 3, 6, 2, 7, 1):
            delivery(which, step).start()
        kept(which).start()

    loads[2].wait()
    weight_copy.wait_recv()
    project(0, order)
    pass_on(0)
    for c in order:
        row_x(c).wait_recv()
    project(1, order)
    pass_on(1)
    for copy in place_copies:
        copy.wait_recv()
    for c in order:
        row_z(c).wait_recv()
        row_relay(c).start()
    deliver(0)
    project(2, order)
    for pair in (order[:2], order[2:]):
        for c in pair:
            row_relay(c).wait_recv()
        project(3, pair)
        if pair[0] == order[0]:
            pass_on(2)
    pass_on(3)
    deliver(1)

    @pl.loop(0, chunks)
    def _(c):
        to_across(c).wait_send()
        to_sibling(c).wait_send()
        relay(c).wait_send()
        near_copy(c, 0).wait_send()
        near_copy(c, 1).wait_send()
        far_copy(c).wait_send()
        row_x(c).wait_send()
        row_z(c).wait_send()
        row_relay(c).wait_send()

    weight_copy.wait_send()
    for copy in place_copies:
        copy.wait_send()
    for k in range(4):
        term_near(k, 0).wait_send()
        term_near(k, 1).wait_send()
        term_far(k).wait_send()
    for which in range(2):
        kept(which).wait()
        for step in range(1, 8):
            delivery(which, step).wait()


def block_body(
    tokens, attn_gain, qkv_weight, out_weight, merge_gain, merge_weight,
    grid_sizes, segment_ids, patch_pos, live_mask, owners,
):
    group_len = segment_ids.shape[0]
    local_rows, width = tokens.shape
    head_width = qkv_weight.shape[1]
    heads_here = head_width // HD
    tok_count = lax.axis_size("tok")
    owned = local_rows // 4
    half = merge_weight.shape[1]
    slot_count = 2 * owned // tok_count
    dma, vmem = pltpu.SemaphoreType.DMA, pltpu.VMEM

    segments, key_live = segment_ids, live_mask
    places = patch_pos.astype(jnp.float32)
    image_count = grid_sizes.shape[1]
    local_image = segments - lax.axis_index("tok") * image_count
    image_match = local_image[:, None] == jnp.arange(image_count, dtype=jnp.int32)[None, :]
    grid_float = grid_sizes.astype(jnp.float32)
    row_size = jnp.sum(jnp.where(image_match, grid_float[0][None, :], 0.0), axis=1)
    col_size = jnp.sum(jnp.where(image_match, grid_float[1][None, :], 0.0), axis=1)
    row_coord = places[0] * SIDE / row_size
    col_coord = places[1] * SIDE / col_size
    segment_float = local_image.astype(jnp.float32)
    lanes = jnp.stack([row_coord, col_coord, segment_float, jnp.zeros_like(row_coord)])
    columns = jnp.stack([segment_float, key_live.astype(jnp.float32)], axis=1)
    quarter = HD // 4
    frequency = 10000.0 ** (-jnp.arange(quarter, dtype=jnp.float32) / quarter)
    fourth = jnp.arange(HD, dtype=jnp.int32) // quarter
    turns = jnp.stack(
        [
            jnp.tile(frequency, 4),
            (fourth // 2).astype(jnp.float32),
            (2 * (fourth % 2) - 1).astype(jnp.float32),
        ],
        axis=1,
    )

    owner_col = owners[:, 0]
    target = (owner_col * (2 * slot_count) + earlier_rows(owner_col)).astype(jnp.float32)
    target = jnp.broadcast_to(jnp.pad(target, (0, 128 - owned))[None, :], (8, 128))

    hbm = pl.BlockSpec(memory_space=pl.ANY)
    delivered = pl.pallas_call(
        layer_kernel,
        out_shape=jax.ShapeDtypeStruct((2, tok_count, 2 * slot_count, 2 * half), jnp.bfloat16),
        in_specs=[VMEM_SPEC] * 7 + [hbm] * 3,
        out_specs=VMEM_SPEC,
        scratch_shapes=[
            vmem((3, head_width, width), jnp.bfloat16),
            vmem((head_width, width), jnp.bfloat16),
            vmem((width, half), jnp.bfloat16),
            vmem((width, half), jnp.bfloat16),
            vmem((3, 4, owned, width), jnp.bfloat16),
            vmem((4, owned, width), jnp.bfloat16),
            vmem((4, owned, width), jnp.bfloat16),
            vmem((heads_here, HD, group_len), jnp.bfloat16),
            vmem((heads_here, group_len, HD), jnp.bfloat16),
            vmem((heads_here, HD, group_len), jnp.bfloat16),
            vmem((2, HD, group_len), jnp.float32),
            vmem((4, 4, owned, width), jnp.bfloat16),
            vmem((2, 4, owned, width), jnp.bfloat16),
            vmem((4, owned, width), jnp.bfloat16),
            vmem((4, owned, width), jnp.bfloat16),
            vmem((4, 4, owned, width), jnp.bfloat16),
            vmem((4, 4, owned, 2 * half), jnp.bfloat16),
            vmem((4, 2, owned, 2 * half), jnp.bfloat16),
            vmem((4, owned, 2 * half), jnp.bfloat16),
            vmem((4, owned, 2 * half), jnp.bfloat16),
            vmem((3, 8, 128), jnp.float32),
            vmem((2, tok_count, 2 * slot_count, 2 * half), jnp.bfloat16),
            dma((3,)), dma((2,)), dma((2, 4)), dma((2, 4)), dma((2, 4)),
            dma((2, 2, 4)), dma((2, 4)), dma((2, 4)), dma((2, 4)), dma((2, 4)),
            dma((2, 4, 2)), dma((2, 4)), dma((2, 3)), dma((2, 2, tok_count)), dma((2,)),
        ],
        compiler_params=pltpu.CompilerParams(
            collective_id=0, has_side_effects=True, vmem_limit_bytes=VMEM_LIMIT
        ),
    )(
        tokens.reshape(4, owned, width), attn_gain, merge_gain, turns, lanes, columns, target,
        qkv_weight, out_weight, merge_weight,
    )
    delivered = delivered.reshape(2, 2, 2, 2, 2, slot_count, 2, half)
    return delivered.transpose(0, 2, 4, 5, 1, 6, 3, 7).reshape(tok_count * slot_count, -1)


def solution(mesh):
    fits_blocks = mesh.shape["head"] == 4 and mesh.shape["tok"] == 8
    placed = (
        P(("tok", "head"), None),
        P(),
        P(None, "head", None),
        P("head", None),
        P(),
        P("head", "tok"),
        P(None, "tok"),
        P("tok"),
        P(None, "tok"),
        P("tok"),
        P(("tok", "head"), None),
    )
    return jax.shard_map(
        block_body if fits_blocks else body, mesh=mesh, in_specs=placed, out_specs=P(("tok", "head"), None), check_vma=False
    )
```
